32 devices in a mesh: lat: 8 (over y, x, core), lev: 4 (over z).
Axes of the slice: x: 2, y: 2, z: 4, core: 2. Of those that a mesh axis runs over, the one named last changes fastest.
Arguments:
- grid: bfloat16 [16, 1024, 2, 2, 8, 128], P(None, 'lat', None, None, None, 'lev'), may hold values from -6 to 6
- legendre: bfloat16 [16, 2, 1024, 512], P('lat'), may hold values from -0.1875 to 0.1875
- quad_weights: float32 [1024], P('lat'), may hold values from 0.25 to 4
- cycle_points: int32 [1024], P('lat'), may hold values from 20 to 4116, as said below
- wave_ids: int32 [16], replicated, may hold values from 0 to 1023, as said below
- mode_projection: bfloat16 [128, 128], replicated, may hold values from -0.5 to 0.5
- vertical_modes: bfloat16 [128, 128], replicated, may hold values from -0.5 to 0.5
- mode_rates: float32 [128], replicated, may hold values from 0.05 to 5
Outputs:
- grid_out: bfloat16 [16, 1024, 2, 2, 8, 128], P(None, 'lat', None, None, None, 'lev')
The draws below stay inside these ranges and needn't reach their ends.
Inputs may be any that keep to these rules, and one draw needn't show every extreme that they name: `cycle_points`: nondecreasing from the first cycle pair to the last; the first cycle pair has the fewest points and the last the most. `wave_ids`: slots 2 i and 2 i + 1 carry wavenumbers m and 1023 - m; no wavenumber appears twice.
All inputs are finite; a program needn't handle non-finite values.
Results may differ from the reference program's by a relative error of at most 0.0073.
Values may be sent and summed in bfloat16 or wider, within the bound.
No kernel may reach another device: no remote copies, remote signals or barrier semaphores. Data moves between devices by JAX's collectives and lax.ppermute only.
A program may use at most 64 MiB of HBM per device.

```python
import math
import jax
import jax.numpy as jnp
from jax import lax

HALF = 1024
MODES = 1024
LEVELS = 128
FIELDS = 8
KHALF = 512
SLOTS = 16


def draw_cycle_points(key, part):
    drawn = jax.random.randint(key, (HALF,), 20, 4 * HALF + 21)
    ordered = jnp.sort(drawn)
    ordered = ordered.at[0].set(20)
    ordered = ordered.at[HALF - 1].set(4 * HALF + 20)
    return ordered.astype(jnp.int32)


def draw_wave_ids(key, part):
    pick_key = jax.random.fold_in(key, 11)
    order_key = jax.random.fold_in(key, 23)
    others = 1 + jax.random.permutation(pick_key, MODES // 2 - 1)[:SLOTS // 2 - 1]
    lower_half = jnp.concatenate([jnp.zeros((1,), jnp.int32), others.astype(jnp.int32)])
    lower_half = lower_half[jax.random.permutation(order_key, SLOTS // 2)]
    paired = jnp.stack([lower_half, MODES - 1 - lower_half], axis=1)
    return paired.reshape(SLOTS).astype(jnp.int32)


def steps_of(key, dims, cuts, low, largest):
    gain = 1.0
    for position, shards_of in cuts:
        heights = jax.random.uniform(jax.random.fold_in(jax.random.fold_in(key, 6), position), (shards_of,), jnp.float32, low / len(cuts), largest / len(cuts))
        gain = gain * jnp.repeat(jnp.exp(heights), dims[position] // shards_of).reshape((-1,) + (1,) * (len(dims) - 1 - position))
    return gain


def noise(stream_key, dims, width, most, shards=(), kind=jnp.bfloat16):
    level = steps_of(stream_key, dims, shards, -0.22, 0.18) if shards else 1.0
    values = jax.random.normal(stream_key, dims, jnp.float32) * width * level
    return jnp.minimum(jnp.maximum(values, -most), most).astype(kind)


def setup_inputs(seed: int = 0) -> dict:
    key_of = jax.random.split(jax.random.key(seed), 9)
    grid = noise(key_of[0], (SLOTS, HALF, 2, 2, FIELDS, LEVELS), 1.0, 6.0, ((1, 8), (5, 4)))
    legendre = noise(key_of[1], (SLOTS, 2, HALF, KHALF), HALF ** -0.5, 0.1875, ((0, 8),))
    quad_weights = jnp.clip(jnp.exp(math.log(4.0) - 2.7725887 * jax.random.uniform(key_of[2], (HALF,), jnp.float32) ** steps_of(key_of[2], (HALF,), ((0, 8),), -0.2, 0.2)), 0.25, 4.0)
    cycle_points = draw_cycle_points(jax.random.fold_in(key_of[8], 71), 0)
    wave_ids = draw_wave_ids(jax.random.fold_in(key_of[8], 71), 0)
    mode_projection = noise(key_of[5], (LEVELS, LEVELS), LEVELS ** -0.5, 0.5)
    vertical_modes = noise(key_of[6], (LEVELS, LEVELS), LEVELS ** -0.5, 0.5)
    mode_rates = jnp.clip(jnp.exp(jax.random.uniform(key_of[7], (LEVELS,), jnp.float32, math.log(0.05), math.log(5.0))), 0.05, 5.0)
    return {"grid": grid, "legendre": legendre, "quad_weights": quad_weights, "cycle_points": cycle_points, "wave_ids": wave_ids, "mode_projection": mode_projection, "vertical_modes": vertical_modes, "mode_rates": mode_rates}


coupling = 2.0


def reference(grid, legendre, quad_weights, cycle_points, wave_ids, mode_projection, vertical_modes, mode_rates):
    def one_slot(operands):
        cycle_slab, leg_table, wave_id = operands
        present = (2 * wave_id < cycle_points).astype(jnp.float32)
        weighting = (quad_weights * present)[:, None, None, None]
        north_cycle = cycle_slab[:, 0].astype(jnp.float32)
        south_cycle = cycle_slab[:, 1].astype(jnp.float32)
        even_part = (weighting * (north_cycle + south_cycle)).astype(jnp.bfloat16)
        odd_part = (weighting * (north_cycle - south_cycle)).astype(jnp.bfloat16)
        folded = jnp.stack([even_part, odd_part]).reshape(2, HALF, 2 * FIELDS * LEVELS)
        k_index = jnp.arange(KHALF, dtype=jnp.int32)
        parity = jnp.arange(2, dtype=jnp.int32)
        total_order = wave_id + parity[:, None] + 2 * k_index[None, :]
        inside = total_order <= MODES - 1
        spectral = jnp.einsum("pjk,pjc->pkc", leg_table.astype(jnp.float32), folded.astype(jnp.float32))
        spectral = jnp.where(inside[:, :, None], spectral, 0.0).astype(jnp.bfloat16)
        spectral = spectral.reshape(2, KHALF, 2, FIELDS, LEVELS)
        projected = jnp.einsum("pkcfl,ql->pkcfq", spectral.astype(jnp.float32), mode_projection.astype(jnp.float32))
        order_float = total_order.astype(jnp.float32)
        growth = coupling * order_float * (order_float + 1.0) / (MODES * MODES)
        damped = (projected / (1.0 + growth[:, :, None, None, None] * mode_rates)).astype(jnp.bfloat16)
        solved = jnp.einsum("pkcfq,lq->pkcfl", damped.astype(jnp.float32), vertical_modes.astype(jnp.float32)).astype(jnp.bfloat16)
        returned = jnp.einsum("pjk,pkc->pjc", leg_table.astype(jnp.float32), solved.reshape(2, KHALF, 2 * FIELDS * LEVELS).astype(jnp.float32)).astype(jnp.bfloat16)
        even_back = returned[0].astype(jnp.float32)
        odd_back = returned[1].astype(jnp.float32)
        north_out = present[:, None] * (even_back + odd_back)
        south_out = present[:, None] * (even_back - odd_back)
        return jnp.stack([north_out, south_out], axis=1).reshape(HALF, 2, 2, FIELDS, LEVELS).astype(jnp.bfloat16)

    return lax.map(one_slot, (grid, legendre, wave_ids))
```

```python
import functools

import jax
import jax.numpy as jnp
from jax import lax
from jax.experimental import pallas as pl
from jax.experimental.pallas import tpu as pltpu
from jax.sharding import PartitionSpec as P

coupling = 2.0
LANES = 128
VMEM_BYTES = 48 * 1024 * 1024


def packed_counts(wave_a, wave_b, parity, modes):
    count_a = lax.shift_right_arithmetic(modes + 1 - wave_a - parity, 1)
    count_b = lax.shift_right_arithmetic(modes + 1 - wave_b - parity, 1)
    return count_a, count_b


def table_kernel(cut, meta, wave, leg, table0, table1, back0, back1):
    lat_n, width, k_half = cut["lat"], cut["cycles"], leg.shape[3]
    me = meta[0]
    modes = 2 * k_half
    wave_a, wave_b = wave[2 * me], wave[2 * me + 1]
    for parity, (table, back) in enumerate(((table0, back0), (table1, back1))):
        kk = table.shape[1]
        count_a, count_b = packed_counts(wave_a, wave_b, parity, modes)
        for slot in range(2):
            shift = 0 if slot == 0 else count_a
            count = count_a if slot == 0 else count_b
            row = lax.broadcasted_iota(jnp.int32, (k_half, kk), 0)
            col = lax.broadcasted_iota(jnp.int32, (k_half, kk), 1)
            pick = jnp.where((col == row + shift) & (row < count), 1.0, 0.0).astype(jnp.bfloat16)
            row_t = lax.broadcasted_iota(jnp.int32, (kk, k_half), 1)
            col_t = lax.broadcasted_iota(jnp.int32, (kk, k_half), 0)
            pick_t = jnp.where((col_t == row_t + shift) & (row_t < count), 1.0, 0.0).astype(
                jnp.bfloat16
            )

            @pl.loop(0, lat_n)
            def _(step):
                owner = jnp.bitwise_xor(me, step)
                block = leg[slot, parity, pl.ds(pl.multiple_of(owner * width, width), width), :]
                start = pl.multiple_of(slot * lat_n * width + step * width, width)
                table[pl.ds(start, width), :] = jnp.dot(
                    block, pick, preferred_element_type=jnp.float32
                ).astype(jnp.bfloat16)
                back[:, pl.ds(start, width)] = lax.dot_general(
                    pick_t, block, (((1,), (1,)), ((), ())), preferred_element_type=jnp.float32
                ).astype(jnp.bfloat16)


def fold_kernel(cut, row0, meta, wave, quad, cycles, grid, *refs):
    lat_n = cut["lat"]
    outs, held, sems = refs[:lat_n], refs[lat_n], refs[lat_n + 1]
    rows = held.shape[3]
    me = meta[0]
    copies = []
    for step in range(lat_n):
        owner = jnp.bitwise_xor(me, step)
        copy = pltpu.make_async_copy(
            grid.at[pl.ds(2 * owner, 2), :, pl.ds(row0, rows), :], held.at[step], sems.at[step]
        )
        copy.start()
        copies.append(copy)
    for step in range(lat_n):
        owner = jnp.bitwise_xor(me, step)
        copies[step].wait()
        for slot in range(2):
            weight = jnp.where(2 * wave[2 * owner + slot] < cycles[...], quad[...], 0.0)
            north = held[step, slot, 0].astype(jnp.float32)
            south = held[step, slot, 1].astype(jnp.float32)
            outs[step][slot, 0] = (weight * (north + south)).astype(jnp.bfloat16)
            outs[step][slot, 1] = (weight * (north - south)).astype(jnp.bfloat16)


def forward_kernel(cut, meta, table0, table1, *refs):
    lat_n, lev_n = cut["lat"], cut["lev"]
    parts, outs, packed = refs[:lat_n], refs[lat_n : lat_n + lev_n], refs[lat_n + lev_n]
    share = outs[0].shape[0]
    at = 0
    for parity, table in enumerate((table0, table1)):
        kk = table.shape[1]
        values = jnp.concatenate(
            [parts[step][slot, parity] for slot in range(2) for step in range(lat_n)], axis=1
        )
        packed[:, at : at + kk] = jnp.dot(
            values, table[...], preferred_element_type=jnp.float32
        ).astype(jnp.bfloat16)
        at += kk
    for step in range(lev_n):
        owner = jnp.bitwise_xor(meta[1], step)
        outs[step][...] = packed[pl.ds(pl.multiple_of(owner * share, share), share), :]


def solve_kernel(cut, meta, wave, project, modes_back, rates, *refs):
    lev_n, levels, k_half, kk0 = cut["lev"], cut["levels"], cut["k_half"], cut["kk"][0]
    parts, outs = refs[:lev_n], refs[lev_n:]
    rows, kk_all = parts[0].shape
    me = meta[0]
    modes = 2 * k_half
    wave_a, wave_b = wave[2 * me], wave[2 * me + 1]
    column = lax.broadcasted_iota(jnp.int32, (8, kk_all), 1)
    odd = column >= kk0
    counts = [packed_counts(wave_a, wave_b, parity, modes) for parity in range(2)]
    count_a = jnp.where(odd, counts[1][0], counts[0][0])
    count_b = jnp.where(odd, counts[1][1], counts[0][1])
    parity = jnp.where(odd, 1, 0)
    place = jnp.where(odd, column - kk0, column)
    order = parity + jnp.where(
        place < count_a, wave_a + 2 * place, wave_b + 2 * (place - count_a)
    )
    order = jnp.where(place < count_a + count_b, order, 0).astype(jnp.float32)
    growth = (coupling * order * (order + 1.0) / (modes * modes))[:1]
    damping = 1.0 + growth * rates[...]
    for col in range(rows // levels):
        at = slice(col * levels, (col + 1) * levels)
        values = jnp.concatenate([parts[step][at, :] for step in range(lev_n)], axis=0)
        projected = jnp.dot(project[...], values, preferred_element_type=jnp.float32)
        damped = (projected / damping).astype(jnp.bfloat16)
        solved = jnp.dot(modes_back[...], damped, preferred_element_type=jnp.float32)
        solved = solved.astype(jnp.bfloat16)
        for step in range(lev_n):
            outs[step][at, :] = solved[step * levels : (step + 1) * levels]


def inverse_kernel(cut, meta, back0, back1, *refs):
    lat_n, lev_n, width = cut["lat"], cut["lev"], cut["cycles"]
    parts, outs, packed = refs[:lev_n], refs[lev_n : lev_n + lat_n], refs[lev_n + lat_n]
    share = parts[0].shape[0]
    for step in range(lev_n):
        owner = jnp.bitwise_xor(meta[1], step)
        packed[pl.ds(pl.multiple_of(owner * share, share), share), :] = parts[step][...]
    at = 0
    for parity, back in enumerate((back0, back1)):
        kk = back.shape[0]
        returned = jnp.dot(
            packed[:, at : at + kk], back[...], preferred_element_type=jnp.float32
        ).astype(jnp.bfloat16)
        for slot in range(2):
            for step in range(lat_n):
                start = (slot * lat_n + step) * width
                outs[step][slot, parity] = returned[:, start : start + width]
        at += kk


def unfold_kernel(cut, row0, chained, meta, wave, cycles, *refs):
    lat_n = cut["lat"]
    parts = refs[:lat_n]
    out, held, sems = refs[lat_n + (1 if chained else 0) :]
    rows = held.shape[3]
    me = meta[0]
    copies = []
    for step in range(lat_n):
        owner = jnp.bitwise_xor(me, step)
        for slot in range(2):
            seen = 2 * wave[2 * owner + slot] < cycles[...]
            even = parts[step][slot, 0].astype(jnp.float32)
            odd = parts[step][slot, 1].astype(jnp.float32)
            held[step, slot, 0] = jnp.where(seen, even + odd, 0.0).astype(jnp.bfloat16)
            held[step, slot, 1] = jnp.where(seen, even - odd, 0.0).astype(jnp.bfloat16)
        copy = pltpu.make_async_copy(
            held.at[step], out.at[pl.ds(2 * owner, 2), :, pl.ds(row0, rows), :], sems.at[step]
        )
        copy.start()
        copies.append(copy)
    for copy in copies:
        copy.wait()


vmem = pl.BlockSpec(memory_space=pltpu.VMEM)
smem = pl.BlockSpec(memory_space=pltpu.SMEM)
anywhere = pl.BlockSpec(memory_space=pl.ANY)


def call(body, name, ins, in_specs, outs, out_specs, scratch, flops=0, aliases=None):
    moved = sum(x.size * x.dtype.itemsize for x in list(ins) + list(outs))
    return pl.pallas_call(
        body,
        name=name,
        out_shape=list(outs),
        in_specs=list(in_specs),
        out_specs=list(out_specs),
        scratch_shapes=list(scratch),
        input_output_aliases=aliases or {},
        cost_estimate=pl.CostEstimate(flops=flops, bytes_accessed=moved, transcendentals=0),
        compiler_params=pltpu.CompilerParams(vmem_limit_bytes=VMEM_BYTES),
    )(*ins)


def struct(*shape):
    return jax.ShapeDtypeStruct(shape, jnp.bfloat16)


def exchange(parts, axis, count):
    return [parts[0]] + [
        lax.ppermute(parts[r], axis, [(i, i ^ r) for i in range(count)]) for r in range(1, count)
    ]


def reordered(array, owner, count, axis):
    size = array.shape[axis] // count
    return jnp.concatenate(
        [
            lax.dynamic_slice_in_dim(array, jnp.bitwise_xor(owner, r) * size, size, axis)
            for r in range(count)
        ],
        axis=axis,
    )


def blocks_of(cols, lev_n):
    pieces = 2
    while pieces > 1 and cols % (pieces * lev_n):
        pieces //= 2
    return [(p * cols // pieces, cols // pieces) for p in range(pieces)]


def local_packed(
    lat_n, lev_n, grid, legendre, quad, cycle_points, wave_ids, projection, vertical, rates
):
    slots, width, halves, parts_c, fields, levels = grid.shape
    k_half = legendre.shape[3]
    cols = parts_c * fields
    kk = (-(-(k_half + 1) // LANES) * LANES, k_half)
    kk_all = sum(kk)
    wide = 2 * lat_n * width
    cut = {
        "lat": lat_n,
        "lev": lev_n,
        "cycles": width,
        "levels": levels,
        "k_half": k_half,
        "kk": kk,
    }
    me_lat, me_lev = lax.axis_index("lat"), lax.axis_index("lev")
    meta = jnp.stack([me_lat, me_lev]).astype(jnp.int32)
    lines = jnp.transpose(grid, (0, 2, 3, 4, 5, 1)).reshape(slots, halves, cols * levels, width)
    quad_row, cycle_row = quad.reshape(1, width), cycle_points.reshape(1, width)
    rates_col = rates.reshape(-1, 1)
    project = reordered(projection, me_lev, lev_n, 1)
    modes_back = reordered(vertical, me_lev, lev_n, 0)

    blocks = blocks_of(cols, lev_n)
    arrived = []
    for first, count in blocks:
        rows = count * levels
        folded = call(
            functools.partial(fold_kernel, cut, first * levels),
            "fold",
            (meta, wave_ids, quad_row, cycle_row, lines),
            (smem, smem, vmem, vmem, anywhere),
            [struct(2, 2, rows, width)] * lat_n,
            [vmem] * lat_n,
            [
                pltpu.VMEM((lat_n, 2, 2, rows, width), jnp.bfloat16),
                pltpu.SemaphoreType.DMA((lat_n,)),
            ],
        )
        arrived.append(exchange(folded, "lat", lat_n))

    table0, table1, back0, back1 = call(
        functools.partial(table_kernel, cut),
        "tables",
        (meta, wave_ids, legendre),
        (smem, smem, vmem),
        [struct(wide, kk[0]), struct(wide, kk[1]), struct(kk[0], wide), struct(kk[1], wide)],
        [vmem] * 4,
        [],
        flops=4 * wide * k_half * kk_all,
    )

    out = None
    for (first, count), parts in zip(blocks, arrived):
        rows = count * levels
        share = rows // lev_n
        flops = 2 * rows * wide * kk_all
        packed = call(
            functools.partial(forward_kernel, cut),
            "forward",
            (meta, table0, table1, *parts),
            [smem] + [vmem] * (2 + lat_n),
            [struct(share, kk_all)] * lev_n,
            [vmem] * lev_n,
            [pltpu.VMEM((rows, kk_all), jnp.bfloat16)],
            flops=flops,
        )
        packed = exchange(packed, "lev", lev_n)
        solved = call(
            functools.partial(solve_kernel, cut),
            "solve",
            (meta, wave_ids, project, modes_back, rates_col, *packed),
            [smem] * 2 + [vmem] * (3 + lev_n),
            [struct(share, kk_all)] * lev_n,
            [vmem] * lev_n,
            [],
            flops=4 * share * lev_n * kk_all * lev_n * levels,
        )
        solved = exchange(solved, "lev", lev_n)
        returned = call(
            functools.partial(inverse_kernel, cut),
            "inverse",
            (meta, back0, back1, *solved),
            [smem] + [vmem] * (2 + lev_n),
            [struct(2, 2, rows, width)] * lat_n,
            [vmem] * lat_n,
            [pltpu.VMEM((rows, kk_all), jnp.bfloat16)],
            flops=flops,
        )
        returned = exchange(returned, "lat", lat_n)
        chained = out is not None
        (out,) = call(
            functools.partial(unfold_kernel, cut, first * levels, chained),
            "unfold",
            (meta, wave_ids, cycle_row, *returned) + ((out,) if chained else ()),
            [smem] * 2 + [vmem] * (1 + lat_n) + ([anywhere] if chained else []),
            [struct(slots, halves, cols * levels, width)],
            [anywhere],
            [
                pltpu.VMEM((lat_n, 2, 2, rows, width), jnp.bfloat16),
                pltpu.SemaphoreType.DMA((lat_n,)),
            ],
            aliases={3 + lat_n: 0} if chained else None,
        )
    out = out.reshape(slots, halves, parts_c, fields, levels, width)
    return jnp.transpose(out, (0, 5, 1, 2, 3, 4))


def local_plain(
    lat_n, lev_n, grid, legendre, quad, cycle_points, wave_ids, projection, vertical, rates
):
    slots, width = grid.shape[:2]
    fields, levels = grid.shape[4:]
    owned, cycles_all, k_half = legendre.shape[0], legendre.shape[2], legendre.shape[3]
    modes = 2 * k_half
    levels_all = projection.shape[0]
    present = (2 * wave_ids[:, None] < cycle_points[None, :]).astype(jnp.float32)
    weighting = (present * quad[None, :])[:, :, None, None, None]
    north, south = grid[:, :, 0].astype(jnp.float32), grid[:, :, 1].astype(jnp.float32)
    even = (weighting * (north + south)).astype(jnp.bfloat16)
    odd = (weighting * (north - south)).astype(jnp.bfloat16)
    folded = jnp.stack([even, odd], axis=2).reshape(slots, width, 2, 2 * fields, levels)
    wave_local = lax.dynamic_slice_in_dim(wave_ids, lax.axis_index("lat") * owned, owned)
    order = (
        wave_local[:, None, None]
        + jnp.arange(2, dtype=jnp.int32)[None, :, None]
        + 2 * jnp.arange(k_half, dtype=jnp.int32)[None, None, :]
    )
    values = lax.all_to_all(folded, "lat", split_axis=0, concat_axis=1, tiled=True)
    values = lax.all_to_all(values, "lev", split_axis=3, concat_axis=4, tiled=True)
    mixed = values.shape[3]
    values = values.reshape(owned, cycles_all, 2, -1)
    spectral = jnp.einsum("spjk,sjpc->spkc", legendre, values, preferred_element_type=jnp.float32)
    spectral = jnp.where((order <= modes - 1)[..., None], spectral, 0.0).astype(jnp.bfloat16)
    spectral = spectral.reshape(owned, 2, k_half, mixed, levels_all)
    order = order.astype(jnp.float32)
    growth = (coupling * order * (order + 1.0) / (modes * modes))[..., None, None]
    last = (((4,), (1,)), ((), ()))
    projected = lax.dot_general(spectral, projection, last, preferred_element_type=jnp.float32)
    damped = (projected / (1.0 + growth * rates)).astype(jnp.bfloat16)
    solved = lax.dot_general(damped, vertical, last, preferred_element_type=jnp.float32)
    solved = solved.astype(jnp.bfloat16).reshape(owned, 2, k_half, -1)
    returned = jnp.einsum("spjk,spkc->sjpc", legendre, solved, preferred_element_type=jnp.float32)
    returned = returned.astype(jnp.bfloat16).reshape(owned, cycles_all, 2, mixed, levels_all)
    back = lax.all_to_all(returned, "lat", split_axis=1, concat_axis=0, tiled=True)
    back = lax.all_to_all(back, "lev", split_axis=4, concat_axis=3, tiled=True)
    back = back.reshape(slots, width, 2, 2, fields, levels).astype(jnp.float32)
    seen = present[:, :, None, None, None]
    north, south = seen * (back[:, :, 0] + back[:, :, 1]), seen * (back[:, :, 0] - back[:, :, 1])
    return jnp.stack([north, south], axis=2).astype(jnp.bfloat16)


def local(lat_n, lev_n, grid, legendre, *rest):
    width, levels = grid.shape[1], grid.shape[5]
    fits = (
        legendre.shape[0] == 2
        and lat_n & (lat_n - 1) == 0
        and lev_n & (lev_n - 1) == 0
        and width % LANES == 0
        and legendre.shape[3] % LANES == 0
        and levels % 16 == 0
        and (grid.shape[3] * grid.shape[4]) % lev_n == 0
    )
    step = local_packed if fits else local_plain
    return step(lat_n, lev_n, grid, legendre, *rest)


def solution(mesh):
    placed = P(None, "lat", None, None, None, "lev")
    return jax.shard_map(
        functools.partial(local, mesh.shape["lat"], mesh.shape["lev"]),
        mesh=mesh,
        in_specs=(placed, P("lat", None, None, None), P("lat"), P("lat"), P(), P(), P(), P()),
        out_specs=placed,
        check_vma=False,
    )
```

```python
import functools

import jax
import jax.numpy as jnp
from jax import lax
from jax.experimental import pallas as pl
from jax.experimental.pallas import tpu as pltpu
from jax.sharding import PartitionSpec as P

coupling = 2.0
LANES = 128
VMEM_BYTES = 48 * 1024 * 1024


def packed_counts(wave_a, wave_b, parity, modes):
    count_a = lax.shift_right_arithmetic(modes + 1 - wave_a - parity, 1)
    count_b = lax.shift_right_arithmetic(modes + 1 - wave_b - parity, 1)
    return count_a, count_b


def table_kernel(cut, wave, leg, *refs):
    lat_n, width, k_half = cut["lat"], cut["cycles"], leg.shape[3]
    table0, table1 = refs[-2:]
    me = lax.axis_index("lat")
    modes = 2 * k_half
    wave_a, wave_b = wave[2 * me], wave[2 * me + 1]
    for parity, table in enumerate((table0, table1)):
        kk = table.shape[1]
        count_a, count_b = packed_counts(wave_a, wave_b, parity, modes)
        row = lax.broadcasted_iota(jnp.int32, (k_half, kk), 0)
        col = lax.broadcasted_iota(jnp.int32, (k_half, kk), 1)
        pick = jnp.where((col == row + count_a) & (row < count_b), 1.0, 0.0).astype(jnp.bfloat16)
        kept = lax.broadcasted_iota(jnp.int32, (width, k_half), 1) < count_a
        blocks = []
        for step in range(lat_n):
            owner = jnp.bitwise_xor(me, step)
            place = pl.ds(pl.multiple_of(owner * width, width), width)
            first = jnp.where(kept, leg[0, parity, place, :].astype(jnp.float32), 0.0)
            table[step * width : (step + 1) * width, :k_half] = first.astype(jnp.bfloat16)
            if kk > k_half:
                table[step * width : (step + 1) * width, k_half:] = jnp.zeros(
                    (width, kk - k_half), jnp.bfloat16
                )
            blocks.append(leg[1, parity, place, :])
        table[lat_n * width :, :] = jnp.dot(
            jnp.concatenate(blocks, axis=0), pick, preferred_element_type=jnp.float32
        ).astype(jnp.bfloat16)


def fold_kernel(cut, row0, wave_in, quad_in, cycles_in, grid, *refs):
    lat_n = cut["lat"]
    outs = refs[-6 - lat_n // 2 : -6]
    held, wave, quad, cycles, sems, small = refs[-6:]
    rows = held.shape[3]
    me = lax.axis_index("lat")
    copies = [
        pltpu.make_async_copy(wave_in, wave, small.at[0]),
        pltpu.make_async_copy(quad_in, quad, small.at[1]),
        pltpu.make_async_copy(cycles_in, cycles, small.at[2]),
    ]
    for step in range(lat_n):
        owner = jnp.bitwise_xor(me, step)
        copies.append(
            pltpu.make_async_copy(
                grid.at[pl.ds(2 * owner, 2), :, pl.ds(row0, rows), :],
                held.at[step],
                sems.at[step],
            )
        )
    for copy in copies:
        copy.start()
    for copy in copies[:3]:
        copy.wait()
    for step in range(lat_n):
        owner = jnp.bitwise_xor(me, step)
        copies[3 + step].wait()
        for slot in range(2):
            weight = jnp.where(2 * wave[2 * owner + slot] < cycles[...], quad[...], 0.0)[None]
            north = held[step, slot, 0].astype(jnp.float32)
            south = held[step, slot, 1].astype(jnp.float32)
            outs[step // 2][step % 2, slot, 0] = (weight * (north + south)).astype(jnp.bfloat16)
            outs[step // 2][step % 2, slot, 1] = (weight * (north - south)).astype(jnp.bfloat16)


def in_order(values):
    me, bit = lax.axis_index("lev"), 1
    while bit < len(values):
        turned = jnp.bitwise_and(me, bit) > 0
        values = [jnp.where(turned, values[r ^ bit], values[r]) for r in range(len(values))]
        bit *= 2
    return values


def gather_kernel(cut, *refs):
    parts, out = refs[: cut["lat"] // 2], refs[-1]
    for step, part in enumerate(parts):
        out[step] = part[1]


def forward_kernel(cut, table0, table1, *refs):
    lat_n, lev_n = cut["lat"], cut["lev"]
    near, swapped, outs = refs[: lat_n // 2], refs[lat_n // 2], refs[-lev_n:]
    share = outs[0].shape[0]
    at = 0
    for parity, table in enumerate((table0, table1)):
        kk = table.shape[1]
        values = jnp.concatenate(
            [
                swapped[step // 2, slot, parity] if step % 2 else near[step // 2][0, slot, parity]
                for slot in range(2)
                for step in range(lat_n)
            ],
            axis=1,
        )
        packed = jnp.dot(values, table[...], preferred_element_type=jnp.float32)
        packed = packed.astype(jnp.bfloat16)
        shares = in_order([packed[r * share : (r + 1) * share] for r in range(lev_n)])
        for out, values in zip(outs, shares):
            out[:, at : at + kk] = values
        at += kk


def solve_kernel(cut, wave, project, vertical, rates, *refs):
    lev_n, levels, k_half, kk0 = cut["lev"], cut["levels"], cut["k_half"], cut["kk"][0]
    parts, outs = refs[:lev_n], refs[-lev_n:]
    rows, kk_all = parts[0].shape
    me = lax.axis_index("lat")

    modes = 2 * k_half
    wave_a, wave_b = wave[2 * me], wave[2 * me + 1]
    column = lax.broadcasted_iota(jnp.int32, (8, kk_all), 1)
    odd = column >= kk0
    counts = [packed_counts(wave_a, wave_b, parity, modes) for parity in range(2)]
    count_a = jnp.where(odd, counts[1][0], counts[0][0])
    count_b = jnp.where(odd, counts[1][1], counts[0][1])
    parity = jnp.where(odd, 1, 0)
    place = jnp.where(odd, column - kk0, column)
    order = parity + jnp.where(
        place < count_a, wave_a + 2 * place, wave_b + 2 * (place - count_a)
    )
    order = jnp.where(place < count_a + count_b, order, 0).astype(jnp.float32)
    growth = (coupling * order * (order + 1.0) / (modes * modes))[:1]
    across = jnp.broadcast_to(rates[...].reshape(1, -1), (LANES, rates.shape[0]))
    damping = 1.0 + growth * across.T[:, :1]
    for col in range(rows // levels):
        at = slice(col * levels, (col + 1) * levels)
        values = in_order([parts[step][at, :] for step in range(lev_n)])
        projected = jnp.dot(
            project[...], jnp.concatenate(values, axis=0), preferred_element_type=jnp.float32
        )
        damped = (projected / damping).astype(jnp.bfloat16)
        solved = jnp.dot(
            vertical[...], damped, preferred_element_type=jnp.float32
        ).astype(jnp.bfloat16)
        values = in_order(
            [solved[step * levels : (step + 1) * levels] for step in range(lev_n)]
        )
        for step in range(lev_n):
            outs[step][at, :] = values[step]


def inverse_kernel(cut, table0, table1, *refs):
    lat_n, lev_n, width = cut["lat"], cut["lev"], cut["cycles"]
    parts, near, swapped = refs[:lev_n], refs[-1 - lat_n // 2 : -1], refs[-1]
    at = 0
    for parity, table in enumerate((table0, table1)):
        kk = table.shape[1]
        shares = in_order([part[:, at : at + kk] for part in parts])
        returned = lax.dot_general(
            jnp.concatenate(shares, axis=0),
            table[...],
            (((1,), (1,)), ((), ())),
            preferred_element_type=jnp.float32,
        ).astype(jnp.bfloat16)
        for slot in range(2):
            for step in range(lat_n):
                start = (slot * lat_n + step) * width
                part = returned[:, start : start + width]
                if step % 2:
                    swapped[step // 2, slot, parity] = part
                else:
                    near[step // 2][0, slot, parity] = part
        at += kk


def merge_kernel(cut, swapped, *refs):
    outs = refs[-(cut["lat"] // 2) :]
    for step, out in enumerate(outs):
        out[1] = swapped[step]


def unfold_kernel(cut, row0, wave, cycles, *refs):
    lat_n = cut["lat"]
    parts = refs[: lat_n // 2]
    out, held, sems = refs[-3:]
    rows = held.shape[3]
    me = lax.axis_index("lat")
    copies = []
    for step in range(lat_n):
        owner = jnp.bitwise_xor(me, step)
        for slot in range(2):
            seen = 2 * wave[2 * owner + slot] < cycles[...]
            even = parts[step // 2][step % 2, slot, 0].astype(jnp.float32)
            odd = parts[step // 2][step % 2, slot, 1].astype(jnp.float32)
            held[step, slot, 0] = jnp.where(seen, even + odd, 0.0).astype(jnp.bfloat16)
            held[step, slot, 1] = jnp.where(seen, even - odd, 0.0).astype(jnp.bfloat16)
        copy = pltpu.make_async_copy(
            held.at[step], out.at[pl.ds(2 * owner, 2), :, pl.ds(row0, rows), :], sems.at[step]
        )
        copy.start()
        copies.append(copy)
    for copy in copies:
        copy.wait()


vmem = pl.BlockSpec(memory_space=pltpu.VMEM)
smem = pl.BlockSpec(memory_space=pltpu.SMEM)
anywhere = pl.BlockSpec(memory_space=pl.ANY)
in_hbm = pl.BlockSpec(memory_space=pltpu.HBM)


def call(body, name, ins, in_specs, outs, out_specs, scratch, aliases=None, after=()):
    return pl.pallas_call(
        body,
        name=name,
        out_shape=list(outs),
        in_specs=list(in_specs) + [anywhere] * len(after),
        out_specs=list(out_specs),
        scratch_shapes=list(scratch),
        input_output_aliases=aliases or {},
        cost_estimate=pl.CostEstimate(flops=0, bytes_accessed=0, transcendentals=0),
        compiler_params=pltpu.CompilerParams(vmem_limit_bytes=VMEM_BYTES),
    )(*ins, *after)


def struct(*shape):
    return jax.ShapeDtypeStruct(shape, jnp.bfloat16)


def exchange(parts, axis, count, stride=1):
    return [parts[0]] + [
        lax.ppermute(part, axis, [(i, i ^ (r * stride)) for i in range(count)])
        for r, part in enumerate(parts)
        if r
    ]


def between_levels(parts, count):
    out = [parts[0]]
    for r in range(1, count):
        part = parts[r]
        if r > 2:
            part, out[r - 2] = lax.optimization_barrier((part, out[r - 2]))
        out.append(lax.ppermute(part, "lev", [(i, i ^ r) for i in range(count)]))
    return out


def swap_cores(array, count):
    return lax.ppermute(array, "lat", [(i, i ^ 1) for i in range(count)])


def blocks_of(cols, lev_n):
    pieces = 2
    while pieces > 1 and cols % (pieces * lev_n):
        pieces //= 2
    return [(p * cols // pieces, cols // pieces) for p in range(pieces)]


def local_packed(
    lat_n, lev_n, grid, legendre, quad, cycle_points, wave_ids, projection, vertical, rates
):
    slots, width, halves, parts_c, fields, levels = grid.shape
    k_half = legendre.shape[3]
    cols = parts_c * fields
    kk = (-(-(k_half + 1) // LANES) * LANES, k_half)
    kk_all = sum(kk)
    wide = 2 * lat_n * width
    cut = {
        "lat": lat_n,
        "lev": lev_n,
        "cycles": width,
        "levels": levels,
        "k_half": k_half,
        "kk": kk,
    }
    lines = jnp.transpose(grid, (0, 2, 3, 4, 5, 1)).reshape(slots, halves, cols * levels, width)
    cycle_row = cycle_points.reshape(1, width)

    blocks = blocks_of(cols, lev_n)
    near_n = lat_n // 2
    last = ()
    arrived = []
    for first, count in blocks:
        rows = count * levels
        folded = call(
            functools.partial(fold_kernel, cut, first * levels),
            "fold",
            (wave_ids, quad, cycle_points, lines),
            [in_hbm] * 4,
            [struct(2, 2, 2, rows, width)] * near_n,
            [vmem] * near_n,
            [
                pltpu.VMEM((lat_n, 2, 2, rows, width), jnp.bfloat16),
                pltpu.SMEM((slots,), jnp.int32),
                pltpu.VMEM((width,), jnp.float32),
                pltpu.VMEM((width,), jnp.int32),
                pltpu.SemaphoreType.DMA((lat_n,)),
                pltpu.SemaphoreType.DMA((3,)),
            ],
            after=last,
        )
        last = (folded[0],)
        arrived.append(exchange(folded, "lat", lat_n, 2))

    table0, table1 = call(
        functools.partial(table_kernel, cut),
        "tables",
        (wave_ids, legendre),
        (smem, vmem),
        [struct(wide, kk[0]), struct(wide, kk[1])],
        [vmem] * 2,
        [],
        after=last,
    )
    last = (table1,)

    def forward(block, last):
        rows = blocks[block][1] * levels
        share = rows // lev_n
        near = arrived[block]
        (swapped,) = call(
            functools.partial(gather_kernel, cut),
            "gather",
            near,
            [vmem] * near_n,
            [struct(near_n, 2, 2, rows, width)],
            [vmem],
            [],
            after=last,
        )
        swapped = swap_cores(swapped, lat_n)
        packed = call(
            functools.partial(forward_kernel, cut),
            "forward",
            (table0, table1, *near, swapped),
            [vmem] * (3 + near_n),
            [struct(share, kk_all)] * lev_n,
            [vmem] * lev_n,
            [],
        )
        return between_levels(packed, lev_n), (packed[0],)

    def solve(packed, last):
        share = packed[0].shape[0]
        solved = call(
            functools.partial(solve_kernel, cut),
            "solve",
            (wave_ids, projection, vertical, rates, *packed),
            [smem] + [vmem] * (3 + lev_n),
            [struct(share, kk_all)] * lev_n,
            [vmem] * lev_n,
            [],
            after=last,
        )
        return between_levels(solved, lev_n), (solved[0],)

    def inverse(solved, last):
        rows = solved[0].shape[0] * lev_n
        *near, swapped = call(
            functools.partial(inverse_kernel, cut),
            "inverse",
            (table0, table1, *solved),
            [vmem] * (2 + lev_n),
            [struct(2, 2, 2, rows, width)] * near_n + [struct(near_n, 2, 2, rows, width)],
            [vmem] * (near_n + 1),
            [],
            after=last,
        )
        swapped = swap_cores(swapped, lat_n)
        merged = call(
            functools.partial(merge_kernel, cut),
            "merge",
            (swapped, *near),
            [vmem] * (1 + near_n),
            [struct(2, 2, 2, rows, width)] * near_n,
            [vmem] * near_n,
            [],
            aliases={1 + r: r for r in range(near_n)},
        )
        return exchange(merged, "lat", lat_n, 2), (merged[0],)

    def unfold(block, returned, out):
        rows = blocks[block][1] * levels
        return call(
            functools.partial(unfold_kernel, cut, blocks[block][0] * levels),
            "unfold",
            (wave_ids, cycle_row, *returned) + out,
            [smem] + [vmem] * (1 + near_n) + [anywhere] * len(out),
            [struct(slots, halves, cols * levels, width)],
            [anywhere],
            [
                pltpu.VMEM((lat_n, 2, 2, rows, width), jnp.bfloat16),
                pltpu.SemaphoreType.DMA((lat_n,)),
            ],
            aliases={2 + near_n: 0} if out else None,
        )

    count = len(blocks)
    packed, solved, returned = [None] * count, [None] * count, [None] * count
    for turn in range(count + 2):
        if 0 <= turn - 2:
            before = returned[turn - 3][1:] if turn - 3 >= 0 else []
            returned[turn - 2], last = inverse(solved[turn - 2], (*last, *before))
        if 0 <= turn - 1 < count:
            solved[turn - 1], last = solve(packed[turn - 1], last)
        if turn < count:
            packed[turn], last = forward(turn, last)
    out = ()
    for block in range(count):
        out = tuple(unfold(block, returned[block], out))
    (out,) = out
    out = out.reshape(slots, halves, parts_c, fields, levels, width)
    return jnp.transpose(out, (0, 5, 1, 2, 3, 4))


def local_plain(
    lat_n, lev_n, grid, legendre, quad, cycle_points, wave_ids, projection, vertical, rates
):
    slots, width = grid.shape[:2]
    fields, levels = grid.shape[4:]
    owned, cycles_all, k_half = legendre.shape[0], legendre.shape[2], legendre.shape[3]
    modes = 2 * k_half
    levels_all = projection.shape[0]
    present = (2 * wave_ids[:, None] < cycle_points[None, :]).astype(jnp.float32)
    weighting = (present * quad[None, :])[:, :, None, None, None]
    north, south = grid[:, :, 0].astype(jnp.float32), grid[:, :, 1].astype(jnp.float32)
    even = (weighting * (north + south)).astype(jnp.bfloat16)
    odd = (weighting * (north - south)).astype(jnp.bfloat16)
    folded = jnp.stack([even, odd], axis=2).reshape(slots, width, 2, 2 * fields, levels)
    wave_local = lax.dynamic_slice_in_dim(wave_ids, lax.axis_index("lat") * owned, owned)
    order = (
        wave_local[:, None, None]
        + jnp.arange(2, dtype=jnp.int32)[None, :, None]
        + 2 * jnp.arange(k_half, dtype=jnp.int32)[None, None, :]
    )
    values = lax.all_to_all(folded, "lat", split_axis=0, concat_axis=1, tiled=True)
    values = lax.all_to_all(values, "lev", split_axis=3, concat_axis=4, tiled=True)
    mixed = values.shape[3]
    values = values.reshape(owned, cycles_all, 2, -1)
    spectral = jnp.einsum("spjk,sjpc->spkc", legendre, values, preferred_element_type=jnp.float32)
    spectral = jnp.where((order <= modes - 1)[..., None], spectral, 0.0).astype(jnp.bfloat16)
    spectral = spectral.reshape(owned, 2, k_half, mixed, levels_all)
    order = order.astype(jnp.float32)
    growth = (coupling * order * (order + 1.0) / (modes * modes))[..., None, None]
    last = (((4,), (1,)), ((), ()))
    projected = lax.dot_general(spectral, projection, last, preferred_element_type=jnp.float32)
    damped = (projected / (1.0 + growth * rates)).astype(jnp.bfloat16)
    solved = lax.dot_general(damped, vertical, last, preferred_element_type=jnp.float32)
    solved = solved.astype(jnp.bfloat16).reshape(owned, 2, k_half, -1)
    returned = jnp.einsum("spjk,spkc->sjpc", legendre, solved, preferred_element_type=jnp.float32)
    returned = returned.astype(jnp.bfloat16).reshape(owned, cycles_all, 2, mixed, levels_all)
    back = lax.all_to_all(returned, "lat", split_axis=1, concat_axis=0, tiled=True)
    back = lax.all_to_all(back, "lev", split_axis=4, concat_axis=3, tiled=True)
    back = back.reshape(slots, width, 2, 2, fields, levels).astype(jnp.float32)
    seen = present[:, :, None, None, None]
    north, south = seen * (back[:, :, 0] + back[:, :, 1]), seen * (back[:, :, 0] - back[:, :, 1])
    return jnp.stack([north, south], axis=2).astype(jnp.bfloat16)


def local(lat_n, lev_n, grid, legendre, *rest):
    width, levels = grid.shape[1], grid.shape[5]
    fits = (
        legendre.shape[0] == 2
        and lat_n & (lat_n - 1) == 0
        and lev_n & (lev_n - 1) == 0
        and width % LANES == 0
        and legendre.shape[3] % LANES == 0
        and levels % 16 == 0
        and lev_n * levels % LANES == 0
        and (grid.shape[3] * grid.shape[4]) % lev_n == 0
    )
    step = local_packed if fits else local_plain
    return step(lat_n, lev_n, grid, legendre, *rest)


def solution(mesh):
    placed = P(None, "lat", None, None, None, "lev")
    return jax.shard_map(
        functools.partial(local, mesh.shape["lat"], mesh.shape["lev"]),
        mesh=mesh,
        in_specs=(placed, P("lat", None, None, None), P("lat"), P("lat"), P(), P(), P(), P()),
        out_specs=placed,
        check_vma=False,
    )
```

```python
import functools

import jax
import jax.numpy as jnp
from jax import lax
from jax.experimental import pallas as pl
from jax.experimental.pallas import tpu as pltpu
from jax.sharding import PartitionSpec as P

coupling = 2.0
CFG = {'zc': (2, 2, 2, 2), 'g1': 0, 'i0': 0, 's1': 0, 'i1': 1, 'late': (1, 0), 'vm': 24, 'fvm': 48, 'u': 0}
LANES = 128


def packed_counts(wave_a, wave_b, parity, modes):
    count_a = lax.shift_right_arithmetic(modes + 1 - wave_a - parity, 1)
    count_b = lax.shift_right_arithmetic(modes + 1 - wave_b - parity, 1)
    return count_a, count_b


def table_kernel(cut, wave, leg, *refs):
    lat_n, width, k_half = cut["lat"], cut["cycles"], leg.shape[3]
    table0, table1 = refs[-2:]
    me = lax.axis_index("lat")
    modes = 2 * k_half
    wave_a, wave_b = wave[2 * me], wave[2 * me + 1]
    for parity, table in enumerate((table0, table1)):
        kk = table.shape[1]
        count_a, count_b = packed_counts(wave_a, wave_b, parity, modes)
        row = lax.broadcasted_iota(jnp.int32, (k_half, kk), 0)
        col = lax.broadcasted_iota(jnp.int32, (k_half, kk), 1)
        pick = jnp.where((col == row + count_a) & (row < count_b), 1.0, 0.0).astype(jnp.bfloat16)
        kept = lax.broadcasted_iota(jnp.int32, (width, k_half), 1) < count_a
        blocks = []
        for step in range(lat_n):
            owner = jnp.bitwise_xor(me, step)
            place = pl.ds(pl.multiple_of(owner * width, width), width)
            first = jnp.where(kept, leg[0, parity, place, :].astype(jnp.float32), 0.0)
            table[step * width : (step + 1) * width, :k_half] = first.astype(jnp.bfloat16)
            if kk > k_half:
                table[step * width : (step + 1) * width, k_half:] = jnp.zeros(
                    (width, kk - k_half), jnp.bfloat16
                )
            blocks.append(leg[1, parity, place, :])
        table[lat_n * width :, :] = jnp.dot(
            jnp.concatenate(blocks, axis=0), pick, preferred_element_type=jnp.float32
        ).astype(jnp.bfloat16)


def fold_kernel(cut, row0, late, wave_in, quad_in, cycles_in, grid, *refs):
    lat_n = cut["lat"]
    outs = refs[-6 - lat_n // 2 : -6]
    if not late:
        outs, others = refs[-7 - lat_n // 2 : -7], refs[-7]
    held, wave, quad, cycles, sems, small = refs[-6:]
    rows = held.shape[3]
    me = lax.axis_index("lat")
    copies = [
        pltpu.make_async_copy(wave_in, wave, small.at[0]),
        pltpu.make_async_copy(quad_in, quad, small.at[1]),
        pltpu.make_async_copy(cycles_in, cycles, small.at[2]),
    ]
    for step in range(lat_n):
        owner = jnp.bitwise_xor(me, step)
        copies.append(
            pltpu.make_async_copy(
                grid.at[pl.ds(2 * owner, 2), :, pl.ds(row0, rows), :],
                held.at[step],
                sems.at[step],
            )
        )
    for copy in copies:
        copy.start()
    for copy in copies[:3]:
        copy.wait()
    for step in range(lat_n):
        owner = jnp.bitwise_xor(me, step)
        copies[3 + step].wait()
        for slot in range(2):
            weight = jnp.where(2 * wave[2 * owner + slot] < cycles[...], quad[...], 0.0)[None]
            north = held[step, slot, 0].astype(jnp.float32)
            south = held[step, slot, 1].astype(jnp.float32)
            out = outs[step // 2].at[step % 2]
            if step % 2 and not late:
                out = others.at[step // 2]
            out[slot, 0] = (weight * (north + south)).astype(jnp.bfloat16)
            out[slot, 1] = (weight * (north - south)).astype(jnp.bfloat16)


def in_order(values):
    me, bit = lax.axis_index("lev"), 1
    while bit < len(values):
        turned = jnp.bitwise_and(me, bit) > 0
        values = [jnp.where(turned, values[r ^ bit], values[r]) for r in range(len(values))]
        bit *= 2
    return values


def arrivals(refs, lat_n, late):
    if late:
        return [refs[lat_n // 2].at[r // 2] if r % 2 else refs[r // 2].at[0] for r in range(lat_n)]
    return [refs[r // 2].at[r % 2] for r in range(lat_n)]


def gather_kernel(cut, *refs):
    parts, out = refs[: cut["lat"] // 2], refs[-1]
    for step, part in enumerate(parts):
        out[step] = part[1]


def forward_kernel(cut, late, table0, table1, *refs):
    lat_n, lev_n = cut["lat"], cut["lev"]
    parts, outs = arrivals(refs, lat_n, late), refs[-lev_n:]
    share = outs[0].shape[0]
    at = 0
    for parity, table in enumerate((table0, table1)):
        kk = table.shape[1]
        values = jnp.concatenate(
            [parts[step][slot, parity] for slot in range(2) for step in range(lat_n)], axis=1
        )
        packed = jnp.dot(values, table[...], preferred_element_type=jnp.float32)
        packed = packed.astype(jnp.bfloat16)
        shares = in_order([packed[r * share : (r + 1) * share] for r in range(lev_n)])
        for out, values in zip(outs, shares):
            out[:, at : at + kk] = values
        at += kk


def solve_kernel(cut, wave, project, vertical, rates, *refs):
    lev_n, levels, k_half, kk0 = cut["lev"], cut["levels"], cut["k_half"], cut["kk"][0]
    parts, outs = refs[:lev_n], refs[-lev_n:]
    rows, kk_all = parts[0].shape
    me = lax.axis_index("lat")

    modes = 2 * k_half
    wave_a, wave_b = wave[2 * me], wave[2 * me + 1]
    column = lax.broadcasted_iota(jnp.int32, (8, kk_all), 1)
    odd = column >= kk0
    counts = [packed_counts(wave_a, wave_b, parity, modes) for parity in range(2)]
    count_a = jnp.where(odd, counts[1][0], counts[0][0])
    count_b = jnp.where(odd, counts[1][1], counts[0][1])
    parity = jnp.where(odd, 1, 0)
    place = jnp.where(odd, column - kk0, column)
    order = parity + jnp.where(
        place < count_a, wave_a + 2 * place, wave_b + 2 * (place - count_a)
    )
    order = jnp.where(place < count_a + count_b, order, 0).astype(jnp.float32)
    growth = (coupling * order * (order + 1.0) / (modes * modes))[:1]
    across = jnp.broadcast_to(rates[...].reshape(1, -1), (LANES, rates.shape[0]))
    damping = 1.0 + growth * across.T[:, :1]
    for col in range(rows // levels):
        at = slice(col * levels, (col + 1) * levels)
        values = in_order([parts[step][at, :] for step in range(lev_n)])
        projected = jnp.dot(
            project[...], jnp.concatenate(values, axis=0), preferred_element_type=jnp.float32
        )
        damped = (projected / damping).astype(jnp.bfloat16)
        solved = jnp.dot(
            vertical[...], damped, preferred_element_type=jnp.float32
        ).astype(jnp.bfloat16)
        values = in_order(
            [solved[step * levels : (step + 1) * levels] for step in range(lev_n)]
        )
        for step in range(lev_n):
            outs[step][at, :] = values[step]


def inverse_kernel(cut, late, table0, table1, *refs):
    lat_n, lev_n, width = cut["lat"], cut["lev"], cut["cycles"]
    parts, near, swapped = refs[:lev_n], refs[-1 - lat_n // 2 : -1], refs[-1]
    if late:
        near = refs[-(lat_n // 2) :]
    at = 0
    for parity, table in enumerate((table0, table1)):
        kk = table.shape[1]
        shares = in_order([part[:, at : at + kk] for part in parts])
        returned = lax.dot_general(
            jnp.concatenate(shares, axis=0),
            table[...],
            (((1,), (1,)), ((), ())),
            preferred_element_type=jnp.float32,
        ).astype(jnp.bfloat16)
        for slot in range(2):
            for step in range(lat_n):
                start = (slot * lat_n + step) * width
                part = returned[:, start : start + width]
                if step % 2 and not late:
                    swapped[step // 2, slot, parity] = part
                else:
                    near[step // 2][step % 2, slot, parity] = part
        at += kk


def merge_kernel(cut, swapped, *refs):
    outs = refs[-(cut["lat"] // 2) :]
    for step, out in enumerate(outs):
        out[1] = swapped[step]


def unfold_kernel(cut, row0, late, wave, cycles, *refs):
    lat_n = cut["lat"]
    parts, (out, held, sems) = arrivals(refs, lat_n, late), refs[-3:]
    rows = held.shape[3]
    me = lax.axis_index("lat")
    copies = []
    for step in range(lat_n):
        owner = jnp.bitwise_xor(me, step)
        for slot in range(2):
            seen = 2 * wave[2 * owner + slot] < cycles[...]
            even = parts[step][slot, 0].astype(jnp.float32)
            odd = parts[step][slot, 1].astype(jnp.float32)
            held[step, slot, 0] = jnp.where(seen, even + odd, 0.0).astype(jnp.bfloat16)
            held[step, slot, 1] = jnp.where(seen, even - odd, 0.0).astype(jnp.bfloat16)
        copy = pltpu.make_async_copy(
            held.at[step], out.at[pl.ds(2 * owner, 2), :, pl.ds(row0, rows), :], sems.at[step]
        )
        copy.start()
        copies.append(copy)
    for copy in copies:
        copy.wait()


vmem = pl.BlockSpec(memory_space=pltpu.VMEM)
smem = pl.BlockSpec(memory_space=pltpu.SMEM)
anywhere = pl.BlockSpec(memory_space=pl.ANY)
in_hbm = pl.BlockSpec(memory_space=pltpu.HBM)


def call(body, name, ins, in_specs, outs, out_specs, scratch, aliases=None, after=(), vm=None):
    return pl.pallas_call(
        body,
        name=name,
        out_shape=list(outs),
        in_specs=list(in_specs) + [anywhere] * len(after),
        out_specs=list(out_specs),
        scratch_shapes=list(scratch),
        input_output_aliases=aliases or {},
        cost_estimate=pl.CostEstimate(flops=0, bytes_accessed=0, transcendentals=0),
        compiler_params=pltpu.CompilerParams(vmem_limit_bytes=(vm or CFG["vm"]) * 2**20),
    )(*ins, *after)


def struct(*shape):
    return jax.ShapeDtypeStruct(shape, jnp.bfloat16)


def exchange(parts, axis, count, stride=1):
    return [parts[0]] + [
        lax.ppermute(part, axis, [(i, i ^ (r * stride)) for i in range(count)])
        for r, part in enumerate(parts)
        if r
    ]


def between_levels(parts, count, mode):
    out = [parts[0]] + [None] * (count - 1)
    waits = {0: {}, 1: {3: 1}, 2: {1: 3}, 3: {1: 2}, 4: {3: 2}, 5: {2: 1}}[mode]
    order = sorted(range(1, count), key=lambda r: (r in waits, r))
    for r in order:
        part = parts[r]
        if r in waits:
            part, out[waits[r]] = lax.optimization_barrier((part, out[waits[r]]))
        out[r] = lax.ppermute(part, "lev", [(i, i ^ r) for i in range(count)])
    return out


def swap_cores(array, count):
    return lax.ppermute(array, "lat", [(i, i ^ 1) for i in range(count)])


def blocks_of(cols, lev_n):
    pieces = 2
    while pieces > 1 and cols % (pieces * lev_n):
        pieces //= 2
    return [(p * cols // pieces, cols // pieces) for p in range(pieces)]


def local_packed(
    lat_n, lev_n, grid, legendre, quad, cycle_points, wave_ids, projection, vertical, rates
):
    slots, width, halves, parts_c, fields, levels = grid.shape
    k_half = legendre.shape[3]
    cols = parts_c * fields
    kk = (-(-(k_half + 1) // LANES) * LANES, k_half)
    kk_all = sum(kk)
    wide = 2 * lat_n * width
    cut = {
        "lat": lat_n,
        "lev": lev_n,
        "cycles": width,
        "levels": levels,
        "k_half": k_half,
        "kk": kk,
    }
    lines = jnp.transpose(grid, (0, 2, 3, 4, 5, 1)).reshape(slots, halves, cols * levels, width)
    cycle_row = cycle_points.reshape(1, width)

    blocks = blocks_of(cols, lev_n)
    near_n = lat_n // 2
    lates = [bool(CFG["late"][block]) for block in range(len(blocks))]
    last = ()
    arrived = []

    def swap(near, others):
        return call(
            functools.partial(merge_kernel, cut),
            "merge",
            (swap_cores(others, lat_n), *near),
            [vmem] * (1 + near_n),
            [struct(*part.shape) for part in near],
            [vmem] * near_n,
            [],
            aliases={1 + r: r for r in range(near_n)},
        )

    def gather(near, last):
        (others,) = call(
            functools.partial(gather_kernel, cut),
            "gather",
            near,
            [vmem] * near_n,
            [struct(near_n, *near[0].shape[1:])],
            [vmem],
            [],
            after=last,
        )
        return [*near, swap_cores(others, lat_n)]

    def outgoing(rows, late):
        shapes = [struct(2, 2, 2, rows, width)] * near_n
        return shapes if late else shapes + [struct(near_n, 2, 2, rows, width)]

    for (first, count), late in zip(blocks, lates):
        rows = count * levels
        folded = call(
            functools.partial(fold_kernel, cut, first * levels, late),
            "fold",
            (wave_ids, quad, cycle_points, lines),
            [in_hbm] * 4,
            outgoing(rows, late),
            [vmem] * len(outgoing(rows, late)),
            [
                pltpu.VMEM((lat_n, 2, 2, rows, width), jnp.bfloat16),
                pltpu.SMEM((slots,), jnp.int32),
                pltpu.VMEM((width,), jnp.float32),
                pltpu.VMEM((width,), jnp.int32),
                pltpu.SemaphoreType.DMA((lat_n,)),
                pltpu.SemaphoreType.DMA((3,)),
            ],
            after=last,
            vm=CFG["fvm"],
        )
        last = (folded[0],)
        if not late:
            folded = swap(folded[:near_n], folded[near_n])
        arrived.append(exchange(folded, "lat", lat_n, 2))

    table0, table1 = call(
        functools.partial(table_kernel, cut),
        "tables",
        (wave_ids, legendre),
        (smem, vmem),
        [struct(wide, kk[0]), struct(wide, kk[1])],
        [vmem] * 2,
        [],
        after=last,
    )
    last = (table1,)

    def forward(block, last):
        rows = blocks[block][1] * levels
        share = rows // lev_n
        parts, late = arrived[block], lates[block]
        if late:
            parts, last = gather(parts, last), ()
        packed = call(
            functools.partial(forward_kernel, cut, late),
            "forward",
            (table0, table1, *parts),
            [vmem] * (2 + len(parts)),
            [struct(share, kk_all)] * lev_n,
            [vmem] * lev_n,
            [],
            after=last,
        )
        return between_levels(packed, lev_n, CFG["zc"][2 * block]), (packed[0],)

    def solve(block, packed, last):
        share = packed[0].shape[0]
        solved = call(
            functools.partial(solve_kernel, cut),
            "solve",
            (wave_ids, projection, vertical, rates, *packed),
            [smem] + [vmem] * (3 + lev_n),
            [struct(share, kk_all)] * lev_n,
            [vmem] * lev_n,
            [],
            after=last,
        )
        return between_levels(solved, lev_n, CFG["zc"][2 * block + 1]), (solved[0],)

    def inverse(block, solved, last, hold=()):
        rows = solved[0].shape[0] * lev_n
        late = lates[block]
        returned = call(
            functools.partial(inverse_kernel, cut, late),
            "inverse",
            (table0, table1, *solved),
            [vmem] * (2 + lev_n),
            outgoing(rows, late),
            [vmem] * len(outgoing(rows, late)),
            [],
            after=last,
        )
        last = (returned[0],)
        if not late:
            returned = swap(returned[:near_n], returned[near_n])
        if hold:
            returned = lax.optimization_barrier((*returned, *hold))[: len(returned)]
        return exchange(returned, "lat", lat_n, 2), last

    def unfold(block, returned, out):
        if lates[block]:
            returned = gather(returned, ())
        rows = blocks[block][1] * levels
        return call(
            functools.partial(unfold_kernel, cut, blocks[block][0] * levels, lates[block]),
            "unfold",
            (wave_ids, cycle_row, *returned) + out,
            [smem] + [vmem] * (1 + len(returned)) + [anywhere] * len(out),
            [struct(slots, halves, cols * levels, width)],
            [anywhere],
            [
                pltpu.VMEM((lat_n, 2, 2, rows, width), jnp.bfloat16),
                pltpu.SemaphoreType.DMA((lat_n,)),
            ],
            aliases={2 + len(returned): 0} if out else None,
        )

    count = len(blocks)
    packed, solved, returned = [None] * count, [None] * count, [None] * count
    for turn in range(count + 2):
        if 0 <= turn - 2:
            extra = []
            if turn == 2 and count > 1:
                extra = [packed[1][r] for r in {0: [], 1: [1], 2: [2], 3: [1, 2, 3], 4: [3], 5: [1, 2]}[CFG["i0"]]]
            if turn == 3:
                extra = returned[0][1:] if CFG["i1"] == 1 else []
            hold = returned[0][1:] if turn == 3 and CFG["i1"] == 2 else []
            returned[turn - 2], last = inverse(turn - 2, solved[turn - 2], (*last, *extra), hold)
        if 0 <= turn - 1 < count:
            extra = []
            if turn == 2:
                extra = {0: [], 1: returned[0][1:2], 2: returned[0][2:3], 3: returned[0][1:4]}[CFG["s1"]]
            solved[turn - 1], last = solve(turn - 1, packed[turn - 1], (*last, *extra))
        if turn < count:
            extra = []
            if turn == 1:
                extra = [solved[0][r] for r in {0: [], 1: [1], 2: [2], 3: [1, 2], 4: [3]}[CFG["g1"]]]
            packed[turn], last = forward(turn, (*last, *extra))
    out = ()
    for block in range(count):
        out = tuple(unfold(block, returned[block], out))
    (out,) = out
    out = out.reshape(slots, halves, parts_c, fields, levels, width)
    return jnp.transpose(out, (0, 5, 1, 2, 3, 4))


def local_plain(
    lat_n, lev_n, grid, legendre, quad, cycle_points, wave_ids, projection, vertical, rates
):
    slots, width = grid.shape[:2]
    fields, levels = grid.shape[4:]
    owned, cycles_all, k_half = legendre.shape[0], legendre.shape[2], legendre.shape[3]
    modes = 2 * k_half
    levels_all = projection.shape[0]
    present = (2 * wave_ids[:, None] < cycle_points[None, :]).astype(jnp.float32)
    weighting = (present * quad[None, :])[:, :, None, None, None]
    north, south = grid[:, :, 0].astype(jnp.float32), grid[:, :, 1].astype(jnp.float32)
    even = (weighting * (north + south)).astype(jnp.bfloat16)
    odd = (weighting * (north - south)).astype(jnp.bfloat16)
    folded = jnp.stack([even, odd], axis=2).reshape(slots, width, 2, 2 * fields, levels)
    wave_local = lax.dynamic_slice_in_dim(wave_ids, lax.axis_index("lat") * owned, owned)
    order = (
        wave_local[:, None, None]
        + jnp.arange(2, dtype=jnp.int32)[None, :, None]
        + 2 * jnp.arange(k_half, dtype=jnp.int32)[None, None, :]
    )
    values = lax.all_to_all(folded, "lat", split_axis=0, concat_axis=1, tiled=True)
    values = lax.all_to_all(values, "lev", split_axis=3, concat_axis=4, tiled=True)
    mixed = values.shape[3]
    values = values.reshape(owned, cycles_all, 2, -1)
    spectral = jnp.einsum("spjk,sjpc->spkc", legendre, values, preferred_element_type=jnp.float32)
    spectral = jnp.where((order <= modes - 1)[..., None], spectral, 0.0).astype(jnp.bfloat16)
    spectral = spectral.reshape(owned, 2, k_half, mixed, levels_all)
    order = order.astype(jnp.float32)
    growth = (coupling * order * (order + 1.0) / (modes * modes))[..., None, None]
    last = (((4,), (1,)), ((), ()))
    projected = lax.dot_general(spectral, projection, last, preferred_element_type=jnp.float32)
    damped = (projected / (1.0 + growth * rates)).astype(jnp.bfloat16)
    solved = lax.dot_general(damped, vertical, last, preferred_element_type=jnp.float32)
    solved = solved.astype(jnp.bfloat16).reshape(owned, 2, k_half, -1)
    returned = jnp.einsum("spjk,spkc->sjpc", legendre, solved, preferred_element_type=jnp.float32)
    returned = returned.astype(jnp.bfloat16).reshape(owned, cycles_all, 2, mixed, levels_all)
    back = lax.all_to_all(returned, "lat", split_axis=1, concat_axis=0, tiled=True)
    back = lax.all_to_all(back, "lev", split_axis=4, concat_axis=3, tiled=True)
    back = back.reshape(slots, width, 2, 2, fields, levels).astype(jnp.float32)
    seen = present[:, :, None, None, None]
    north, south = seen * (back[:, :, 0] + back[:, :, 1]), seen * (back[:, :, 0] - back[:, :, 1])
    return jnp.stack([north, south], axis=2).astype(jnp.bfloat16)


def local(lat_n, lev_n, grid, legendre, *rest):
    width, levels = grid.shape[1], grid.shape[5]
    fits = (
        legendre.shape[0] == 2
        and lat_n & (lat_n - 1) == 0
        and lev_n & (lev_n - 1) == 0
        and width % LANES == 0
        and legendre.shape[3] % LANES == 0
        and levels % 16 == 0
        and lev_n * levels % LANES == 0
        and (grid.shape[3] * grid.shape[4]) % lev_n == 0
    )
    step = local_packed if fits else local_plain
    return step(lat_n, lev_n, grid, legendre, *rest)


def solution(mesh):
    placed = P(None, "lat", None, None, None, "lev")
    return jax.shard_map(
        functools.partial(local, mesh.shape["lat"], mesh.shape["lev"]),
        mesh=mesh,
        in_specs=(placed, P("lat", None, None, None), P("lat"), P("lat"), P(), P(), P(), P()),
        out_specs=placed,
        check_vma=False,
    )
```

```python
import functools

import jax
import jax.numpy as jnp
from jax import lax
from jax.experimental import pallas as pl
from jax.experimental.pallas import tpu as pltpu
from jax.sharding import PartitionSpec as P

coupling = 2.0
VMEM_MIB = 24
FOLD_VMEM_MIB = 48
LANES = 128


def packed_counts(wave_a, wave_b, parity, modes):
    count_a = lax.shift_right_arithmetic(modes + 1 - wave_a - parity, 1)
    count_b = lax.shift_right_arithmetic(modes + 1 - wave_b - parity, 1)
    return count_a, count_b


def table_kernel(cut, wave, leg, *refs):
    lat_n, width, k_half = cut["lat"], cut["cycles"], leg.shape[3]
    table0, table1 = refs[-2:]
    me = lax.axis_index("lat")
    modes = 2 * k_half
    wave_a, wave_b = wave[2 * me], wave[2 * me + 1]
    for parity, table in enumerate((table0, table1)):
        kk = table.shape[1]
        count_a, count_b = packed_counts(wave_a, wave_b, parity, modes)
        row = lax.broadcasted_iota(jnp.int32, (k_half, kk), 0)
        col = lax.broadcasted_iota(jnp.int32, (k_half, kk), 1)
        pick = jnp.where((col == row + count_a) & (row < count_b), 1.0, 0.0).astype(jnp.bfloat16)
        kept = lax.broadcasted_iota(jnp.int32, (width, k_half), 1) < count_a
        blocks = []
        for step in range(lat_n):
            owner = jnp.bitwise_xor(me, step)
            place = pl.ds(pl.multiple_of(owner * width, width), width)
            first = jnp.where(kept, leg[0, parity, place, :].astype(jnp.float32), 0.0)
            table[step * width : (step + 1) * width, :k_half] = first.astype(jnp.bfloat16)
            if kk > k_half:
                table[step * width : (step + 1) * width, k_half:] = jnp.zeros(
                    (width, kk - k_half), jnp.bfloat16
                )
            blocks.append(leg[1, parity, place, :])
        table[lat_n * width :, :] = jnp.dot(
            jnp.concatenate(blocks, axis=0), pick, preferred_element_type=jnp.float32
        ).astype(jnp.bfloat16)


def fold_kernel(cut, row0, late, weights, grid, *refs):
    lat_n = cut["lat"]
    outs = refs[-2 - lat_n // 2 : -2]
    if not late:
        outs, others = refs[-3 - lat_n // 2 : -3], refs[-3]
    held, sems = refs[-2:]
    rows = held.shape[3]
    me = lax.axis_index("lat")
    copies = []
    for step in range(lat_n):
        owner = jnp.bitwise_xor(me, step)
        copies.append(
            pltpu.make_async_copy(
                grid.at[pl.ds(2 * owner, 2), :, pl.ds(row0, rows), :],
                held.at[step],
                sems.at[step],
            )
        )
    for copy in copies:
        copy.start()
    for step in range(lat_n):
        owner = jnp.bitwise_xor(me, step)
        copies[step].wait()
        for slot in range(2):
            weight = weights[pl.ds(2 * owner + slot, 1), :]
            north = held[step, slot, 0].astype(jnp.float32)
            south = held[step, slot, 1].astype(jnp.float32)
            out = outs[step // 2].at[step % 2]
            if step % 2 and not late:
                out = others.at[step // 2]
            out[slot, 0] = (weight * (north + south)).astype(jnp.bfloat16)
            out[slot, 1] = (weight * (north - south)).astype(jnp.bfloat16)


def in_order(values):
    me, bit = lax.axis_index("lev"), 1
    while bit < len(values):
        turned = jnp.bitwise_and(me, bit) > 0
        values = [jnp.where(turned, values[r ^ bit], values[r]) for r in range(len(values))]
        bit *= 2
    return values


def arrivals(refs, lat_n, late):
    if late:
        return [refs[lat_n // 2].at[r // 2] if r % 2 else refs[r // 2].at[0] for r in range(lat_n)]
    return [refs[r // 2].at[r % 2] for r in range(lat_n)]


def gather_kernel(cut, *refs):
    parts, out = refs[: cut["lat"] // 2], refs[-1]
    for step, part in enumerate(parts):
        out[step] = part[1]


def forward_kernel(cut, late, table0, table1, *refs):
    lat_n, lev_n = cut["lat"], cut["lev"]
    parts, outs = arrivals(refs, lat_n, late), refs[-lev_n:]
    share = outs[0].shape[0]
    at = 0
    for parity, table in enumerate((table0, table1)):
        kk = table.shape[1]
        values = jnp.concatenate(
            [parts[step][slot, parity] for slot in range(2) for step in range(lat_n)], axis=1
        )
        packed = jnp.dot(values, table[...], preferred_element_type=jnp.float32)
        packed = packed.astype(jnp.bfloat16)
        shares = in_order([packed[r * share : (r + 1) * share] for r in range(lev_n)])
        for out, values in zip(outs, shares):
            out[:, at : at + kk] = values
        at += kk


def solve_kernel(cut, wave, project, vertical, rates, *refs):
    lev_n, levels, k_half, kk0 = cut["lev"], cut["levels"], cut["k_half"], cut["kk"][0]
    parts, outs = refs[:lev_n], refs[-lev_n:]
    rows, kk_all = parts[0].shape
    me = lax.axis_index("lat")

    modes = 2 * k_half
    wave_a, wave_b = wave[2 * me], wave[2 * me + 1]
    column = lax.broadcasted_iota(jnp.int32, (8, kk_all), 1)
    odd = column >= kk0
    counts = [packed_counts(wave_a, wave_b, parity, modes) for parity in range(2)]
    count_a = jnp.where(odd, counts[1][0], counts[0][0])
    count_b = jnp.where(odd, counts[1][1], counts[0][1])
    parity = jnp.where(odd, 1, 0)
    place = jnp.where(odd, column - kk0, column)
    order = parity + jnp.where(
        place < count_a, wave_a + 2 * place, wave_b + 2 * (place - count_a)
    )
    order = jnp.where(place < count_a + count_b, order, 0).astype(jnp.float32)
    growth = (coupling * order * (order + 1.0) / (modes * modes))[:1]
    across = jnp.broadcast_to(rates[...].reshape(1, -1), (LANES, rates.shape[0]))
    damping = 1.0 + growth * across.T[:, :1]
    for col in range(rows // levels):
        at = slice(col * levels, (col + 1) * levels)
        values = in_order([parts[step][at, :] for step in range(lev_n)])
        projected = jnp.dot(
            project[...], jnp.concatenate(values, axis=0), preferred_element_type=jnp.float32
        )
        damped = (projected / damping).astype(jnp.bfloat16)
        solved = jnp.dot(
            vertical[...], damped, preferred_element_type=jnp.float32
        ).astype(jnp.bfloat16)
        values = in_order(
            [solved[step * levels : (step + 1) * levels] for step in range(lev_n)]
        )
        for step in range(lev_n):
            outs[step][at, :] = values[step]


def inverse_kernel(cut, late, table0, table1, *refs):
    lat_n, lev_n, width = cut["lat"], cut["lev"], cut["cycles"]
    parts, near, swapped = refs[:lev_n], refs[-1 - lat_n // 2 : -1], refs[-1]
    if late:
        near = refs[-(lat_n // 2) :]
    at = 0
    for parity, table in enumerate((table0, table1)):
        kk = table.shape[1]
        shares = in_order([part[:, at : at + kk] for part in parts])
        returned = lax.dot_general(
            jnp.concatenate(shares, axis=0),
            table[...],
            (((1,), (1,)), ((), ())),
            preferred_element_type=jnp.float32,
        ).astype(jnp.bfloat16)
        for slot in range(2):
            for step in range(lat_n):
                start = (slot * lat_n + step) * width
                part = returned[:, start : start + width]
                if step % 2 and not late:
                    swapped[step // 2, slot, parity] = part
                else:
                    near[step // 2][step % 2, slot, parity] = part
        at += kk


def part_kernel(cut, swapped, *outs):
    for step, out in enumerate(outs):
        out[0] = swapped[step]


def merge_kernel(cut, swapped, *refs):
    outs = refs[-(cut["lat"] // 2) :]
    for step, out in enumerate(outs):
        out[1] = swapped[step]


def unfold_kernel(row0, places, wave, cycles, *refs):
    out, held, sems = refs[-3:]
    rows = held.shape[3]
    me = lax.axis_index("lat")
    copies = []
    for step, (r, ref, at) in enumerate(places):
        part = refs[ref].at[at]
        owner = jnp.bitwise_xor(me, r)
        for slot in range(2):
            seen = 2 * wave[2 * owner + slot] < cycles[...]
            even = part[slot, 0].astype(jnp.float32)
            odd = part[slot, 1].astype(jnp.float32)
            held[step, slot, 0] = jnp.where(seen, even + odd, 0.0).astype(jnp.bfloat16)
            held[step, slot, 1] = jnp.where(seen, even - odd, 0.0).astype(jnp.bfloat16)
        copy = pltpu.make_async_copy(
            held.at[step], out.at[pl.ds(2 * owner, 2), :, pl.ds(row0, rows), :], sems.at[step]
        )
        copy.start()
        copies.append(copy)
    for copy in copies:
        copy.wait()


vmem = pl.BlockSpec(memory_space=pltpu.VMEM)
smem = pl.BlockSpec(memory_space=pltpu.SMEM)
anywhere = pl.BlockSpec(memory_space=pl.ANY)
in_hbm = pl.BlockSpec(memory_space=pltpu.HBM)


def call(body, name, ins, in_specs, outs, out_specs, scratch, aliases=None, after=(), vm=None):
    return pl.pallas_call(
        body,
        name=name,
        out_shape=list(outs),
        in_specs=list(in_specs) + [anywhere] * len(after),
        out_specs=list(out_specs),
        scratch_shapes=list(scratch),
        input_output_aliases=aliases or {},
        cost_estimate=pl.CostEstimate(flops=0, bytes_accessed=0, transcendentals=0),
        compiler_params=pltpu.CompilerParams(vmem_limit_bytes=(vm or VMEM_MIB) * 2**20),
    )(*ins, *after)


def struct(*shape):
    return jax.ShapeDtypeStruct(shape, jnp.bfloat16)


def exchange(parts, axis, count, stride=1):
    return [parts[0]] + [
        lax.ppermute(part, axis, [(i, i ^ (r * stride)) for i in range(count)])
        for r, part in enumerate(parts)
        if r
    ]


def between_levels(parts, count, chained):
    out = [parts[0]] + [None] * (count - 1)
    for r in list(range(2, count)) + [1]:
        part = parts[r]
        if r == 1 and chained and count > 2:
            part, out[count - 1] = lax.optimization_barrier((part, out[count - 1]))
        out[r] = lax.ppermute(part, "lev", [(i, i ^ r) for i in range(count)])
    return out


def swap_cores(array, count):
    return lax.ppermute(array, "lat", [(i, i ^ 1) for i in range(count)])


def blocks_of(cols, lev_n):
    pieces = 1 if cols % (2 * lev_n) else 2
    return [(p * cols // pieces, cols // pieces) for p in range(pieces)]


def local_packed(
    lat_n, lev_n, grid, legendre, quad, cycle_points, wave_ids, projection, vertical, rates
):
    slots, width, halves, parts_c, fields, levels = grid.shape
    k_half = legendre.shape[3]
    cols = parts_c * fields
    kk = (-(-(k_half + 1) // LANES) * LANES, k_half)
    kk_all = sum(kk)
    wide = 2 * lat_n * width
    cut = {
        "lat": lat_n,
        "lev": lev_n,
        "cycles": width,
        "levels": levels,
        "k_half": k_half,
        "kk": kk,
    }
    lines = jnp.transpose(grid, (0, 2, 3, 4, 5, 1)).reshape(slots, halves, cols * levels, width)
    present = wave_ids[:, None] < cycle_points[None, :] - wave_ids[:, None]
    weights = jnp.where(present, quad[None, :], 0.0)
    cycle_row = cycle_points.reshape(1, width)

    blocks = blocks_of(cols, lev_n)
    near_n = lat_n // 2
    lates = [block == 0 for block in range(len(blocks))]
    last = ()
    arrived = []

    def swap(near, others):
        return call(
            functools.partial(merge_kernel, cut),
            "merge",
            (swap_cores(others, lat_n), *near),
            [vmem] * (1 + near_n),
            [struct(*part.shape) for part in near],
            [vmem] * near_n,
            [],
            aliases={1 + r: r for r in range(near_n)},
        )

    def gather(near, last):
        (others,) = call(
            functools.partial(gather_kernel, cut),
            "gather",
            near,
            [vmem] * near_n,
            [struct(near_n, *near[0].shape[1:])],
            [vmem],
            [],
            after=last,
        )
        return [*near, swap_cores(others, lat_n)]

    def outgoing(rows, late, split=False):
        shapes = [struct(1 if split else 2, 2, 2, rows, width)] * near_n
        return shapes if late else shapes + [struct(near_n, 2, 2, rows, width)]

    for (first, count), late in zip(blocks, lates):
        rows = count * levels
        folded = call(
            functools.partial(fold_kernel, cut, first * levels, late),
            "fold",
            (weights, lines),
            [vmem, in_hbm],
            outgoing(rows, late),
            [vmem] * len(outgoing(rows, late)),
            [
                pltpu.VMEM((lat_n, 2, 2, rows, width), jnp.bfloat16),
                pltpu.SemaphoreType.DMA((lat_n,)),
            ],
            after=last,
            vm=FOLD_VMEM_MIB,
        )
        last = (folded[0],)
        if not late:
            folded = swap(folded[:near_n], folded[near_n])
        arrived.append(exchange(folded, "lat", lat_n, 2))

    table0, table1 = call(
        functools.partial(table_kernel, cut),
        "tables",
        (wave_ids, legendre),
        (smem, vmem),
        [struct(wide, kk[0]), struct(wide, kk[1])],
        [vmem] * 2,
        [],
        after=last,
    )
    last = (table1,)

    def forward(block, last):
        rows = blocks[block][1] * levels
        share = rows // lev_n
        parts, late = arrived[block], lates[block]
        if late:
            parts, last = gather(parts, last), ()
        packed = call(
            functools.partial(forward_kernel, cut, late),
            "forward",
            (table0, table1, *parts),
            [vmem] * (2 + len(parts)),
            [struct(share, kk_all)] * lev_n,
            [vmem] * lev_n,
            [],
            after=last,
        )
        return between_levels(packed, lev_n, True), (packed[0],)

    def solve(block, packed, last):
        share = packed[0].shape[0]
        solved = call(
            functools.partial(solve_kernel, cut),
            "solve",
            (wave_ids, projection, vertical, rates, *packed),
            [smem] + [vmem] * (3 + lev_n),
            [struct(share, kk_all)] * lev_n,
            [vmem] * lev_n,
            [],
            after=last,
        )
        return between_levels(solved, lev_n, block == 0), (solved[0],)

    def inverse(block, solved, last):
        rows = solved[0].shape[0] * lev_n
        late = lates[block]
        returned = call(
            functools.partial(inverse_kernel, cut, late),
            "inverse",
            (table0, table1, *solved),
            [vmem] * (2 + lev_n),
            outgoing(rows, late, not late),
            [vmem] * len(outgoing(rows, late)),
            [],
            after=last,
        )
        last = (returned[0],)
        mine = exchange(returned[:near_n], "lat", lat_n, 2)
        if late:
            return mine, last
        others = call(
            functools.partial(part_kernel, cut),
            "part",
            (swap_cores(returned[near_n], lat_n),),
            [vmem],
            [struct(1, 2, 2, rows, width)] * near_n,
            [vmem] * near_n,
            [],
        )
        others = exchange(others, "lat", lat_n, 2)
        return [part for pair in zip(mine, others) for part in pair], last

    def unfold(block, returned, out):
        early = lat_n
        if lates[block]:
            returned = gather(returned, ())
            places = [(r, near_n, r // 2) if r % 2 else (r, r // 2, 0) for r in range(lat_n)]
        else:
            places = [(r, r, 0) for r in range(lat_n)]
            early = 3 * lat_n // 4
        rows = blocks[block][1] * levels
        for part in (places[:early], places[early:]):
            if not part:
                continue
            used = sorted({ref for _, ref, _ in part})
            part = [(r, used.index(ref), at) for r, ref, at in part]
            out = call(
                functools.partial(unfold_kernel, blocks[block][0] * levels, part),
                "unfold",
                (wave_ids, cycle_row, *[returned[ref] for ref in used], *out),
                [smem] + [vmem] * (1 + len(used)) + [anywhere] * len(out),
                [struct(slots, halves, cols * levels, width)],
                [anywhere],
                [
                    pltpu.VMEM((len(part), 2, 2, rows, width), jnp.bfloat16),
                    pltpu.SemaphoreType.DMA((len(part),)),
                ],
                aliases={2 + len(used): 0} if out else None,
            )
        return out

    count = len(blocks)
    out = ()
    packed, solved, returned = [None] * count, [None] * count, [None] * count
    for turn in range(count + 2):
        if 0 <= turn - 2:
            sent = returned[turn - 3][1:] if turn >= 3 else ()
            returned[turn - 2], last = inverse(turn - 2, solved[turn - 2], (*last, *sent))
        if 0 <= turn - 1 < count:
            solved[turn - 1], last = solve(turn - 1, packed[turn - 1], last)
        if turn < count:
            packed[turn], last = forward(turn, last)
    for block in range(count):
        out = tuple(unfold(block, returned[block], out))
    (out,) = out
    out = out.reshape(slots, halves, parts_c, fields, levels, width)
    return jnp.transpose(out, (0, 5, 1, 2, 3, 4))


def local_plain(
    lat_n, lev_n, grid, legendre, quad, cycle_points, wave_ids, projection, vertical, rates
):
    slots, width = grid.shape[:2]
    fields, levels = grid.shape[4:]
    owned, cycles_all, k_half = legendre.shape[0], legendre.shape[2], legendre.shape[3]
    modes = 2 * k_half
    levels_all = projection.shape[0]
    present = (2 * wave_ids[:, None] < cycle_points[None, :]).astype(jnp.float32)
    weighting = (present * quad[None, :])[:, :, None, None, None]
    north, south = grid[:, :, 0].astype(jnp.float32), grid[:, :, 1].astype(jnp.float32)
    even = (weighting * (north + south)).astype(jnp.bfloat16)
    odd = (weighting * (north - south)).astype(jnp.bfloat16)
    folded = jnp.stack([even, odd], axis=2).reshape(slots, width, 2, 2 * fields, levels)
    wave_local = lax.dynamic_slice_in_dim(wave_ids, lax.axis_index("lat") * owned, owned)
    order = (
        wave_local[:, None, None]
        + jnp.arange(2, dtype=jnp.int32)[None, :, None]
        + 2 * jnp.arange(k_half, dtype=jnp.int32)[None, None, :]
    )
    values = lax.all_to_all(folded, "lat", split_axis=0, concat_axis=1, tiled=True)
    values = lax.all_to_all(values, "lev", split_axis=3, concat_axis=4, tiled=True)
    mixed = values.shape[3]
    values = values.reshape(owned, cycles_all, 2, -1)
    spectral = jnp.einsum("spjk,sjpc->spkc", legendre, values, preferred_element_type=jnp.float32)
    spectral = jnp.where((order <= modes - 1)[..., None], spectral, 0.0).astype(jnp.bfloat16)
    spectral = spectral.reshape(owned, 2, k_half, mixed, levels_all)
    order = order.astype(jnp.float32)
    growth = (coupling * order * (order + 1.0) / (modes * modes))[..., None, None]
    last = (((4,), (1,)), ((), ()))
    projected = lax.dot_general(spectral, projection, last, preferred_element_type=jnp.float32)
    damped = (projected / (1.0 + growth * rates)).astype(jnp.bfloat16)
    solved = lax.dot_general(damped, vertical, last, preferred_element_type=jnp.float32)
    solved = solved.astype(jnp.bfloat16).reshape(owned, 2, k_half, -1)
    returned = jnp.einsum("spjk,spkc->sjpc", legendre, solved, preferred_element_type=jnp.float32)
    returned = returned.astype(jnp.bfloat16).reshape(owned, cycles_all, 2, mixed, levels_all)
    back = lax.all_to_all(returned, "lat", split_axis=1, concat_axis=0, tiled=True)
    back = lax.all_to_all(back, "lev", split_axis=4, concat_axis=3, tiled=True)
    back = back.reshape(slots, width, 2, 2, fields, levels).astype(jnp.float32)
    seen = present[:, :, None, None, None]
    north, south = seen * (back[:, :, 0] + back[:, :, 1]), seen * (back[:, :, 0] - back[:, :, 1])
    return jnp.stack([north, south], axis=2).astype(jnp.bfloat16)


def local(lat_n, lev_n, grid, legendre, *rest):
    width, levels = grid.shape[1], grid.shape[5]
    fits = (
        legendre.shape[0] == 2
        and lat_n & (lat_n - 1) == 0
        and lev_n & (lev_n - 1) == 0
        and width % LANES == 0
        and legendre.shape[3] % LANES == 0
        and levels % 16 == 0
        and lev_n * levels % LANES == 0
        and (grid.shape[3] * grid.shape[4]) % lev_n == 0
    )
    step = local_packed if fits else local_plain
    return step(lat_n, lev_n, grid, legendre, *rest)


def solution(mesh):
    placed = P(None, "lat", None, None, None, "lev")
    return jax.shard_map(
        functools.partial(local, mesh.shape["lat"], mesh.shape["lev"]),
        mesh=mesh,
        in_specs=(placed, P("lat", None, None, None), P("lat"), P("lat"), P(), P(), P(), P()),
        out_specs=placed,
        check_vma=False,
    )
```
